32 devices in a mesh: tile: 8 (over y, x, core), lag: 4 (over z).
Axes of the slice: x: 2, y: 2, z: 4, core: 2. Of those that a mesh axis runs over, the one named last changes fastest.
Arguments:
- history: bfloat16 [8, 64, 384, 512], P('lag', 'tile'), may hold values from -6 to 6
- lag_blocks: bfloat16 [8, 64, 2, 384, 384], P('lag', 'tile'), may hold values from -0.09375 to 0.09375
- self_inverse: bfloat16 [64, 384, 384], P('tile'), may hold values from -0.3125 to 0.3125
- excitation: float32 [64, 384, 512], P('tile'), may hold values from -6 to 6
- pattern: int32 [8, 64, 2], P('lag', 'tile'), may hold values from 0 to 8
- live_counts: int32 [8, 64], P('lag', 'tile'), may hold values from 1 to 2
Outputs:
- traction: bfloat16 [64, 384, 512], P('tile')
- shifted_history: bfloat16 [8, 64, 384, 512], P('lag', 'tile')
The draws below stay inside these ranges and needn't reach their ends.
All inputs are finite; a program needn't handle non-finite values.
Results may differ from the reference program's by a relative error of at most 0.013.
Values may be sent and summed in bfloat16 or wider, within the bound.
A program may use at most 128 MiB of HBM per device.

```python
import jax
import jax.numpy as jnp
from jax import lax

VEC = 384
LAG_DEV = 2
EXCITE = 512
SLOTS = 2
EDGE = 4
BLOCKS = 64
LAGS = 8
N_LAG = 4


def draw_pattern(key, part):
    width = 2 * EDGE + 1
    first_key, second_key = jax.random.split(jax.random.fold_in(key, 11))
    base = jax.random.randint(first_key, (LAGS, BLOCKS, 1), 0, width, dtype=jnp.int32)
    stride = jax.random.randint(second_key, (LAGS, BLOCKS, 1), 1, width, dtype=jnp.int32)
    row_ids = jnp.arange(LAGS, dtype=jnp.int32)[:, None, None] * BLOCKS + jnp.arange(BLOCKS, dtype=jnp.int32)[None, :, None]
    base = jnp.where(row_ids == 0, width - 1, base)
    base = jnp.where(row_ids == 1, 0, base)
    slot_ids = jnp.arange(SLOTS, dtype=jnp.int32)[None, None, :]
    return ((base + slot_ids * stride) % width).astype(jnp.int32)


def place_ends(values, stream_key, least, largest):
    index_at = [jax.random.randint(jax.random.fold_in(stream_key, axis), (), 0, length) for axis, length in enumerate(values.shape)]
    main_axis = values.shape.index(max(values.shape))
    next_to = index_at[:main_axis] + [(index_at[main_axis] + 1) % values.shape[main_axis]] + index_at[main_axis + 1:]
    return values.at[tuple(index_at)].set(least).at[tuple(next_to)].set(largest)


def block_levels(stream_key, dims, cuts, least, high):
    level = 1.0
    for position, parts in cuts:
        draws = jax.random.uniform(jax.random.fold_in(jax.random.fold_in(stream_key, 6), position), (parts,), jnp.float32, least / len(cuts), high / len(cuts))
        level = level * jnp.repeat(jnp.exp(draws), dims[position] // parts).reshape((-1,) + (1,) * (len(dims) - 1 - position))
    return level


def bell_draw(rng, dims, scale, bound, shards=(), kind=jnp.bfloat16):
    result = scale * jax.random.normal(rng, dims, jnp.float32)
    if shards:
        result = result * block_levels(rng, dims, shards, -0.22, 0.18)
    return jnp.clip(result, -bound, bound).astype(kind)


def setup_inputs(seed: int = 0) -> dict:
    arg_keys = jax.random.split(jax.random.key(seed), 7)
    return {
        "history": bell_draw(arg_keys[0], (LAGS, BLOCKS, VEC, EXCITE), 1.0, 6.0, ((0, 4), (1, 8))),
        "lag_blocks": bell_draw(arg_keys[1], (LAGS, BLOCKS, SLOTS, VEC, VEC), (VEC * LAGS * 3 // 2) ** -0.5, 0.09375, ((0, 4), (1, 8))),
        "self_inverse": bell_draw(arg_keys[2], (BLOCKS, VEC, VEC), VEC ** -0.5, 0.3125, ((0, 8),)),
        "excitation": bell_draw(arg_keys[3], (BLOCKS, VEC, EXCITE), 1.0, 6.0, ((0, 8),), jnp.float32),
        "pattern": draw_pattern(jax.random.fold_in(arg_keys[6], 71), 0),
        "live_counts": place_ends(jax.random.randint(arg_keys[5], (LAGS, BLOCKS), 1, SLOTS + 1), jax.random.fold_in(arg_keys[5], 1), 1, SLOTS).astype(jnp.int32),
    }


def lag_term(history, lag_blocks, pattern, live_counts, lag):
    positions = jnp.arange(BLOCKS, dtype=jnp.int32)
    source_index = (positions[:, None] + pattern[lag] - EDGE) % BLOCKS
    live = jnp.arange(SLOTS, dtype=jnp.int32)[None, :] < live_counts[lag][:, None]
    sources = history[lag][source_index] * live[:, :, None, None].astype(history.dtype)
    return jnp.einsum("bsij,bsjr->bir", lag_blocks[lag].astype(jnp.float32), sources.astype(jnp.float32))


def reference(history, lag_blocks, self_inverse, excitation, pattern, live_counts):
    def group_term(group):
        def one_lag(offset):
            return lag_term(history, lag_blocks, pattern, live_counts, group * LAG_DEV + offset)
        terms = lax.map(one_lag, jnp.arange(LAG_DEV, dtype=jnp.int32))
        return jnp.sum(terms, axis=0).astype(jnp.bfloat16)

    partials = lax.map(group_term, jnp.arange(N_LAG, dtype=jnp.int32))
    field = jnp.sum(partials.astype(jnp.float32), axis=0)
    residual = (excitation - field).astype(jnp.bfloat16)
    traction = jnp.einsum("bij,bjr->bir", self_inverse.astype(jnp.float32), residual.astype(jnp.float32)).astype(jnp.bfloat16)
    shifted_history = jnp.concatenate([traction[None], history[:-1]], axis=0)
    return (traction, shifted_history)
```

```python
import functools

import jax
import jax.numpy as jnp
from jax import lax
from jax.experimental import pallas as pl
from jax.experimental.pallas import tpu as pltpu
from jax.sharding import PartitionSpec as P

SLOTS = 2
EDGE = 4
COLS = 256
ROWS = 128
MESH = pl.DeviceIdType.MESH


def march(
    n_tile, n_lag,
    history, lag_blocks, self_inverse, excitation, pattern, live_counts,
    traction, shifted,
    window, land, blocks, inverse, excite, psend, inbox, resbox, tbuf,
    local_sem, halo_send, halo_recv, carry_send, carry_recv,
    in_send, in_recv, res_send, res_recv, out_sem, first_sem,
):
    lags, here, vec, width = history.shape
    tile = lax.axis_index("tile")
    lag = lax.axis_index("lag")
    half = n_lag // 2
    right, left = lax.rem(tile + 1, n_tile), lax.rem(tile + n_tile - 1, n_tile)
    left_half = lag < half
    inward = jnp.where(left_half, lag + 1, lag - 1)
    has_out = (lag > 0) & (lag < n_lag - 1)
    outward = jnp.where(has_out, jnp.where(left_half, lag - 1, lag + 1), inward)
    middle = (lag == half - 1) | (lag == half)

    def halo(k, side):
        block = here - 1 - k if side == 0 else k
        return pltpu.make_async_remote_copy(
            src_ref=history.at[:, block],
            dst_ref=land.at[k, side],
            send_sem=halo_send.at[k, side],
            recv_sem=halo_recv.at[k, side],
            device_id={"tile": right if side == 0 else left},
            device_id_type=MESH,
        )

    def carry(c):
        return pltpu.make_async_remote_copy(
            src_ref=history.at[lags - 1, c],
            dst_ref=shifted.at[0, c],
            send_sem=carry_send.at[c],
            recv_sem=carry_recv.at[c],
            device_id={"lag": lax.rem(lag + 1, n_lag)},
            device_id_type=MESH,
        )

    def to_inward(k, dst, recv):
        return pltpu.make_async_remote_copy(
            src_ref=psend.at[k],
            dst_ref=dst.at[k],
            send_sem=in_send.at[k],
            recv_sem=recv.at[k],
            device_id={"lag": inward},
            device_id_type=MESH,
        )

    def to_outward(k):
        return pltpu.make_async_remote_copy(
            src_ref=resbox.at[k],
            dst_ref=resbox.at[k],
            send_sem=res_send.at[k],
            recv_sem=res_recv.at[k],
            device_id={"lag": outward},
            device_id_type=MESH,
        )

    def target(k, side):
        return EDGE - 1 - k + side * (2 * k + 1)

    barrier = pltpu.get_barrier_semaphore()
    pl.semaphore_signal(barrier, inc=1, device_id={"tile": left}, device_id_type=MESH)
    pl.semaphore_signal(barrier, inc=1, device_id={"tile": right}, device_id_type=MESH)

    @pl.when(lag > 0)
    def _():
        pl.semaphore_signal(barrier, inc=1, device_id={"lag": lag - 1}, device_id_type=MESH)

    @pl.when(lag < n_lag - 1)
    def _():
        pl.semaphore_signal(barrier, inc=1, device_id={"lag": lag + 1}, device_id_type=MESH)

    at_end = (lag == 0) | (lag == n_lag - 1)
    pl.semaphore_wait(barrier, jnp.where(at_end, 3, 4))

    halo(0, 0).start()
    halo(0, 1).start()

    def start_carry(late):
        for c in range(here):
            early = c < 2 * (lag + 1)
            @pl.when((lag < n_lag - 1) & (~early if late else early))
            def _():
                carry(c).start()

    start_carry(False)

    loads = [
        pltpu.make_async_copy(history, window.at[:, pl.ds(EDGE, here)], local_sem.at[0]),
        pltpu.make_async_copy(lag_blocks, blocks, local_sem.at[1]),
        pltpu.make_async_copy(self_inverse, inverse, local_sem.at[2]),
        pltpu.make_async_copy(excitation, excite, local_sem.at[3]),
    ]
    for load in loads:
        load.start()
    for l in range(lags):
        @pl.loop(0, vec // ROWS)
        def _(r):
            window[l, here + 2 * EDGE, pl.ds(pl.multiple_of(r * ROWS, ROWS), ROWS)] = jnp.zeros((ROWS, width), window.dtype)
    for load in loads:
        load.wait()
    kept = pltpu.make_async_copy(
        window.at[pl.ds(0, lags - 1), pl.ds(EDGE, here)], shifted.at[pl.ds(1, lags - 1)], local_sem.at[4]
    )
    kept.start()

    def compute(k):
        halo(k, 0).wait_recv()
        halo(k, 1).wait_recv()
        if k + 1 < EDGE:
            halo(k + 1, 0).start()
            halo(k + 1, 1).start()
        for l in range(lags):
            @pl.loop(0, vec // ROWS)
            def _(r):
                rows = pl.ds(pl.multiple_of(r * ROWS, ROWS), ROWS)
                window[l, EDGE - 1 - k, rows] = land[k, 0, l, rows]
                window[l, EDGE + here + k, rows] = land[k, 1, l, rows]

        @pl.loop(0, 2 * (width // COLS))
        def _(step):
            side = step // (width // COLS)
            cols = pl.ds(pl.multiple_of(lax.rem(step, width // COLS) * COLS, COLS), COLS)
            b = target(k, side)
            lhs, rhs = [], []
            for l in range(lags):
                for s in range(SLOTS):
                    index = jnp.where(s < live_counts[l, b], b + pattern[l, b, s], here + 2 * EDGE)
                    lhs.append(blocks[l, b, s])
                    rhs.append(window[l, index, :, cols])
            term = jnp.dot(
                jnp.concatenate(lhs, axis=1), jnp.concatenate(rhs, axis=0),
                preferred_element_type=jnp.float32,
            )
            psend[k, side, :, cols] = term.astype(psend.dtype)

    def forward(k):
        @pl.when(has_out)
        def _():
            to_inward(k, inbox, in_recv).wait_recv()

            @pl.loop(0, 2 * (vec // ROWS))
            def _(step):
                side = step // (vec // ROWS)
                rows = pl.ds(pl.multiple_of(lax.rem(step, vec // ROWS) * ROWS, ROWS), ROWS)
                psend[k, side, rows] = (
                    psend[k, side, rows].astype(jnp.float32) + inbox[k, side, rows].astype(jnp.float32)
                ).astype(psend.dtype)

        @pl.when(middle)
        def _():
            to_inward(k, resbox, res_recv).start()

        @pl.when(~middle)
        def _():
            to_inward(k, inbox, in_recv).start()

    def resolve(k):
        to_outward(k).wait_recv()

        @pl.when(middle)
        def _():
            @pl.loop(0, 2 * (vec // ROWS))
            def _(step):
                side = step // (vec // ROWS)
                rows = pl.ds(pl.multiple_of(lax.rem(step, vec // ROWS) * ROWS, ROWS), ROWS)
                field = psend[k, side, rows].astype(jnp.float32) + resbox[k, side, rows].astype(jnp.float32)
                resbox[k, side, rows] = (excite[target(k, side), rows] - field).astype(resbox.dtype)

        @pl.when(has_out)
        def _():
            to_outward(k).start()

        @pl.loop(0, 2)
        def _(side):
            tbuf[k, side] = jnp.dot(
                inverse[target(k, side)], resbox[k, side], preferred_element_type=jnp.float32
            ).astype(tbuf.dtype)

        for side in range(2):
            write_out(k, side).start()

            @pl.when(lag == 0)
            def _():
                write_first(k, side).start()

    def write_out(k, side):
        return pltpu.make_async_copy(tbuf.at[k, side], traction.at[target(k, side)], out_sem.at[k, side])

    def write_first(k, side):
        return pltpu.make_async_copy(tbuf.at[k, side], shifted.at[0, target(k, side)], first_sem.at[k, side])

    order = [(compute, 0)]
    for k in range(1, EDGE):
        order += [(compute, k)]
        if k == EDGE - 1:
            order += [(resolve, 0)]
        order += [(forward, k - 1)]
    order += [(resolve, 1), (forward, EDGE - 1)]
    for step, k in order:
        step(k)

    @pl.when(left_half)
    def _():
        start_carry(True)

    for k in range(2, EDGE):
        resolve(k)

    @pl.when(~left_half)
    def _():
        start_carry(True)

    kept.wait()
    for k in range(EDGE):
        for side in range(2):
            halo(k, side).wait_send()
            write_out(k, side).wait()

            @pl.when(lag == 0)
            def _():
                write_first(k, side).wait()

        to_inward(k, inbox, in_recv).wait_send()

        @pl.when(has_out)
        def _():
            to_outward(k).wait_send()

    for c in range(here):
        @pl.when(lag < n_lag - 1)
        def _():
            carry(c).wait_send()

        @pl.when(lag > 0)
        def _():
            carry(c).wait_recv()


def shards(n_tile, n_lag, history, lag_blocks, self_inverse, excitation, pattern, live_counts):
    lags, here, vec, width = history.shape
    kind = history.dtype
    anywhere = pl.BlockSpec(memory_space=pl.ANY)
    scalars = pl.BlockSpec(memory_space=pltpu.SMEM)
    dma = pltpu.SemaphoreType.DMA
    pair = (EDGE, 2, vec, width)
    flops = 2 * here * vec * vec * width * (lags * SLOTS + 1)
    return pl.pallas_call(
        functools.partial(march, n_tile, n_lag),
        out_shape=(
            jax.ShapeDtypeStruct((here, vec, width), kind),
            jax.ShapeDtypeStruct((lags, here, vec, width), kind),
        ),
        in_specs=[anywhere] * 4 + [scalars] * 2,
        out_specs=(anywhere, anywhere),
        scratch_shapes=[
            pltpu.VMEM((lags, here + 2 * EDGE + 1, vec, width), kind),
            pltpu.VMEM((EDGE, 2, lags, vec, width), kind),
            pltpu.VMEM(lag_blocks.shape, kind),
            pltpu.VMEM(self_inverse.shape, kind),
            pltpu.VMEM(excitation.shape, excitation.dtype),
            pltpu.VMEM(pair, kind),
            pltpu.VMEM(pair, kind),
            pltpu.VMEM(pair, kind),
            pltpu.VMEM(pair, kind),
            dma((5,)),
            dma((EDGE, 2)), dma((EDGE, 2)),
            dma((here,)), dma((here,)),
            dma((EDGE,)), dma((EDGE,)),
            dma((EDGE,)), dma((EDGE,)),
            dma((EDGE, 2)), dma((EDGE, 2)),
        ],
        compiler_params=pltpu.CompilerParams(
            collective_id=0, has_side_effects=True, vmem_limit_bytes=60 * 2**20
        ),
        cost_estimate=pl.CostEstimate(flops=flops, bytes_accessed=40 * 2**20, transcendentals=0),
    )(history, lag_blocks, self_inverse, excitation, pattern, live_counts)


def solution(mesh):
    in_specs = (
        P("lag", "tile", None, None),
        P("lag", "tile", None, None, None),
        P("tile", None, None),
        P("tile", None, None),
        P("lag", "tile", None),
        P("lag", "tile"),
    )
    out_specs = (P("tile", None, None), P("lag", "tile", None, None))
    body = functools.partial(shards, mesh.shape["tile"], mesh.shape["lag"])
    return jax.shard_map(body, mesh=mesh, in_specs=in_specs, out_specs=out_specs, check_vma=False)
```

```python
import functools

import jax
import jax.numpy as jnp
from jax import lax
from jax.experimental import pallas as pl
from jax.experimental.pallas import tpu as pltpu
from jax.sharding import PartitionSpec as P

SLOTS = 2
EDGE = 4
COLS = 256
ROWS = 128
MESH = pl.DeviceIdType.MESH


def march(
    n_tile, n_lag,
    history, lag_blocks, self_inverse, excitation, pattern, live_counts,
    traction, shifted,
    window, land, blocks, inverse, excite, psend, inbox, resbox, tbuf,
    local_sem, halo_send, halo_recv, carry_send, carry_recv,
    in_send, in_recv, res_send, res_recv, out_sem, first_sem,
):
    lags, here, vec, width = history.shape
    tile = lax.axis_index("tile")
    lag = lax.axis_index("lag")
    half = n_lag // 2
    right, left = lax.rem(tile + 1, n_tile), lax.rem(tile + n_tile - 1, n_tile)
    left_half = lag < half
    inward = jnp.where(left_half, lag + 1, lag - 1)
    has_out = (lag > 0) & (lag < n_lag - 1)
    outward = jnp.where(has_out, jnp.where(left_half, lag - 1, lag + 1), inward)
    middle = (lag == half - 1) | (lag == half)

    def halo(k, side, l):
        block = here - 1 - k if side == 0 else k
        return pltpu.make_async_remote_copy(
            src_ref=history.at[l, block],
            dst_ref=land.at[k, side, l],
            send_sem=halo_send.at[k, side, l],
            recv_sem=halo_recv.at[k, side, l],
            device_id={"tile": right if side == 0 else left},
            device_id_type=MESH,
        )

    def carry(c):
        return pltpu.make_async_remote_copy(
            src_ref=history.at[lags - 1, c],
            dst_ref=shifted.at[0, c],
            send_sem=carry_send.at[c],
            recv_sem=carry_recv.at[c],
            device_id={"lag": lax.rem(lag + 1, n_lag)},
            device_id_type=MESH,
        )

    def to_inward(k, side, dst, recv):
        return pltpu.make_async_remote_copy(
            src_ref=psend.at[k, side],
            dst_ref=dst.at[k, side],
            send_sem=in_send.at[k, side],
            recv_sem=recv.at[k, side],
            device_id={"lag": inward},
            device_id_type=MESH,
        )

    def to_outward(k, side):
        return pltpu.make_async_remote_copy(
            src_ref=resbox.at[k, side],
            dst_ref=resbox.at[k, side],
            send_sem=res_send.at[k, side],
            recv_sem=res_recv.at[k, side],
            device_id={"lag": outward},
            device_id_type=MESH,
        )

    def target(k, side):
        return EDGE - 1 - k + side * (2 * k + 1)

    barrier = pltpu.get_barrier_semaphore()
    pl.semaphore_signal(barrier, inc=1, device_id={"tile": left}, device_id_type=MESH)
    pl.semaphore_signal(barrier, inc=1, device_id={"tile": right}, device_id_type=MESH)

    @pl.when(lag > 0)
    def _():
        pl.semaphore_signal(barrier, inc=1, device_id={"lag": lag - 1}, device_id_type=MESH)

    @pl.when(lag < n_lag - 1)
    def _():
        pl.semaphore_signal(barrier, inc=1, device_id={"lag": lag + 1}, device_id_type=MESH)

    at_end = (lag == 0) | (lag == n_lag - 1)
    pl.semaphore_wait(barrier, jnp.where(at_end, 3, 4))

    for l in range(lags):
        for side in range(2):
            halo(0, side, l).start()

    def is_early(c):
        return (c < 2 * (lag + 2)) | ~left_half

    for c in range(here):
        @pl.when((lag < n_lag - 1) & is_early(c))
        def _():
            carry(c).start()

    def start_late(part):
        for c in range(part, here, 2):
            @pl.when((lag < n_lag - 1) & ~is_early(c))
            def _():
                carry(c).start()

    loads = [
        pltpu.make_async_copy(history, window.at[:, pl.ds(EDGE, here)], local_sem.at[0]),
        pltpu.make_async_copy(lag_blocks, blocks, local_sem.at[1]),
        pltpu.make_async_copy(self_inverse, inverse, local_sem.at[2]),
        pltpu.make_async_copy(excitation, excite, local_sem.at[3]),
    ]
    for load in loads:
        load.start()
    for l in range(lags):
        @pl.loop(0, vec // ROWS)
        def _(r):
            window[l, here + 2 * EDGE, pl.ds(pl.multiple_of(r * ROWS, ROWS), ROWS)] = jnp.zeros((ROWS, width), window.dtype)
    for load in loads:
        load.wait()
    kept = pltpu.make_async_copy(
        window.at[pl.ds(0, lags - 1), pl.ds(EDGE, here)], shifted.at[pl.ds(1, lags - 1)], local_sem.at[4]
    )
    kept.start()

    def compute(k):
        for l in range(lags):
            for side in range(2):
                halo(k, side, l).wait_recv()
                if k + 1 < EDGE:
                    halo(k + 1, side, l).start()
        for l in range(lags):
            @pl.loop(0, vec // ROWS)
            def _(r):
                rows = pl.ds(pl.multiple_of(r * ROWS, ROWS), ROWS)
                window[l, EDGE - 1 - k, rows] = land[k, 0, l, rows]
                window[l, EDGE + here + k, rows] = land[k, 1, l, rows]

        for side in range(2):
            b = target(k, side)

            @pl.loop(0, width // COLS)
            def _(c):
                cols = pl.ds(pl.multiple_of(c * COLS, COLS), COLS)
                lhs, rhs = [], []
                for l in range(lags):
                    for s in range(SLOTS):
                        index = jnp.where(s < live_counts[l, b], b + pattern[l, s, b], here + 2 * EDGE)
                        lhs.append(blocks[l, b, s])
                        rhs.append(window[l, index, :, cols])
                term = jnp.dot(
                    jnp.concatenate(lhs, axis=1), jnp.concatenate(rhs, axis=0),
                    preferred_element_type=jnp.float32,
                )
                psend[k, side, :, cols] = term.astype(psend.dtype)

            @pl.when(~has_out)
            def _():
                send_inward(k, side)

    def send_inward(k, side):
        @pl.when(middle)
        def _():
            to_inward(k, side, resbox, res_recv).start()

        @pl.when(~middle)
        def _():
            to_inward(k, side, inbox, in_recv).start()

    def forward(k):
        @pl.when(has_out)
        def _():
            for side in range(2):
                to_inward(k, side, inbox, in_recv).wait_recv()

                @pl.loop(0, vec // ROWS)
                def _(r):
                    rows = pl.ds(pl.multiple_of(r * ROWS, ROWS), ROWS)
                    psend[k, side, rows] = (
                        psend[k, side, rows].astype(jnp.float32) + inbox[k, side, rows].astype(jnp.float32)
                    ).astype(psend.dtype)

                send_inward(k, side)

    def resolve(k, side):
        to_outward(k, side).wait_recv()

        @pl.when(middle)
        def _():
            @pl.loop(0, vec // ROWS)
            def _(r):
                rows = pl.ds(pl.multiple_of(r * ROWS, ROWS), ROWS)
                field = psend[k, side, rows].astype(jnp.float32) + resbox[k, side, rows].astype(jnp.float32)
                resbox[k, side, rows] = (excite[target(k, side), rows] - field).astype(resbox.dtype)

        @pl.when(has_out)
        def _():
            to_outward(k, side).start()

        tbuf[k, side] = jnp.dot(
            inverse[target(k, side)], resbox[k, side], preferred_element_type=jnp.float32
        ).astype(tbuf.dtype)
        write_out(k, side).start()

        @pl.when(lag == 0)
        def _():
            write_first(k, side).start()

    def write_out(k, side):
        return pltpu.make_async_copy(tbuf.at[k, side], traction.at[target(k, side)], out_sem.at[k, side])

    def write_first(k, side):
        return pltpu.make_async_copy(tbuf.at[k, side], shifted.at[0, target(k, side)], first_sem.at[k, side])

    def resolve_middle(k):
        @pl.when(middle)
        def _():
            for side in range(2):
                resolve(k, side)
                if k == EDGE - 1:
                    start_late(side)

    for k in range(EDGE):
        if k == EDGE - 1:
            resolve_middle(0)
        compute(k)
        if k > 0:
            forward(k - 1)
    resolve_middle(1)
    forward(EDGE - 1)
    for k in range(2, EDGE):
        resolve_middle(k)

    @pl.when(~middle)
    def _():
        for side in range(2):
            to_inward(EDGE - 1, side, inbox, in_recv).wait_send()
            start_late(side)
        for k in range(EDGE):
            for side in range(2):
                resolve(k, side)

    kept.wait()
    for k in range(EDGE):
        for side in range(2):
            for l in range(lags):
                halo(k, side, l).wait_send()
            write_out(k, side).wait()

            @pl.when(lag == 0)
            def _():
                write_first(k, side).wait()

            if k < EDGE - 1:
                to_inward(k, side, inbox, in_recv).wait_send()
            else:
                @pl.when(middle)
                def _():
                    to_inward(k, side, inbox, in_recv).wait_send()

            @pl.when(has_out)
            def _():
                to_outward(k, side).wait_send()

    for c in range(here):
        @pl.when(lag < n_lag - 1)
        def _():
            carry(c).wait_send()

        @pl.when(lag > 0)
        def _():
            carry(c).wait_recv()


def shards(n_tile, n_lag, history, lag_blocks, self_inverse, excitation, pattern, live_counts):
    lags, here, vec, width = history.shape
    kind = history.dtype
    anywhere = pl.BlockSpec(memory_space=pl.ANY)
    scalars = pl.BlockSpec(memory_space=pltpu.SMEM)
    dma = pltpu.SemaphoreType.DMA
    pair = (EDGE, 2, vec, width)
    flops = 2 * here * vec * vec * width * (lags * SLOTS + 1)
    return pl.pallas_call(
        functools.partial(march, n_tile, n_lag),
        out_shape=(
            jax.ShapeDtypeStruct((here, vec, width), kind),
            jax.ShapeDtypeStruct((lags, here, vec, width), kind),
        ),
        in_specs=[anywhere] * 4 + [scalars] * 2,
        out_specs=(anywhere, anywhere),
        scratch_shapes=[
            pltpu.VMEM((lags, here + 2 * EDGE + 1, vec, width), kind),
            pltpu.VMEM((EDGE, 2, lags, vec, width), kind),
            pltpu.VMEM(lag_blocks.shape, kind),
            pltpu.VMEM(self_inverse.shape, kind),
            pltpu.VMEM(excitation.shape, excitation.dtype),
            pltpu.VMEM(pair, kind),
            pltpu.VMEM(pair, kind),
            pltpu.VMEM(pair, kind),
            pltpu.VMEM(pair, kind),
            dma((5,)),
            dma((EDGE, 2, lags)), dma((EDGE, 2, lags)),
            dma((here,)), dma((here,)),
            dma((EDGE, 2)), dma((EDGE, 2)),
            dma((EDGE, 2)), dma((EDGE, 2)),
            dma((EDGE, 2)), dma((EDGE, 2)),
        ],
        compiler_params=pltpu.CompilerParams(
            collective_id=0, has_side_effects=True, vmem_limit_bytes=60 * 2**20
        ),
        cost_estimate=pl.CostEstimate(flops=flops, bytes_accessed=40 * 2**20, transcendentals=0),
    )(history, lag_blocks, self_inverse, excitation, jnp.swapaxes(pattern, 1, 2), live_counts)


def solution(mesh):
    in_specs = (
        P("lag", "tile", None, None),
        P("lag", "tile", None, None, None),
        P("tile", None, None),
        P("tile", None, None),
        P("lag", "tile", None),
        P("lag", "tile"),
    )
    out_specs = (P("tile", None, None), P("lag", "tile", None, None))
    body = functools.partial(shards, mesh.shape["tile"], mesh.shape["lag"])
    return jax.shard_map(body, mesh=mesh, in_specs=in_specs, out_specs=out_specs, check_vma=False)
```

```python
import functools

import jax
import jax.numpy as jnp
from jax import lax
from jax.experimental import pallas as pl
from jax.experimental.pallas import tpu as pltpu
from jax.sharding import PartitionSpec as P

SLOTS = 2
EDGE = 4
COLS = 256
ROWS = 128
MESH = pl.DeviceIdType.MESH


def march(
    n_tile, n_lag,
    history, lag_blocks, self_inverse, excitation, pattern, live_counts,
    traction, newest, older,
    window, land, blocks, inverse, excite, psend, inbox, resbox,
    local_sem, halo_send, halo_recv, carry_send, carry_recv,
    in_send, in_recv, res_send, res_recv,
):
    lags, here, vec, width = history.shape
    tile = lax.axis_index("tile")
    lag = lax.axis_index("lag")
    half = n_lag // 2
    right, left = lax.rem(tile + 1, n_tile), lax.rem(tile + n_tile - 1, n_tile)
    left_half = lag < half
    inward = jnp.where(left_half, lag + 1, lag - 1)
    has_out = (lag > 0) & (lag < n_lag - 1)
    outward = jnp.where(has_out, jnp.where(left_half, lag - 1, lag + 1), inward)
    middle = (lag == half - 1) | (lag == half)

    def halo(k, side, l):
        block = here - 1 - k if side == 0 else k
        return pltpu.make_async_remote_copy(
            src_ref=history.at[l, block],
            dst_ref=land.at[k, side, l],
            send_sem=halo_send.at[k, side, l],
            recv_sem=halo_recv.at[k, side, l],
            device_id={"tile": right if side == 0 else left},
            device_id_type=MESH,
        )

    def carry(c):
        return pltpu.make_async_remote_copy(
            src_ref=history.at[lags - 1, c],
            dst_ref=newest.at[c],
            send_sem=carry_send.at[c],
            recv_sem=carry_recv.at[c],
            device_id={"lag": lax.rem(lag + 1, n_lag)},
            device_id_type=MESH,
        )

    def to_inward(k, side, dst, recv):
        return pltpu.make_async_remote_copy(
            src_ref=psend.at[k, side],
            dst_ref=dst.at[k, side],
            send_sem=in_send.at[k, side],
            recv_sem=recv.at[k, side],
            device_id={"lag": inward},
            device_id_type=MESH,
        )

    def to_outward(k, side):
        return pltpu.make_async_remote_copy(
            src_ref=resbox.at[k, side],
            dst_ref=resbox.at[k, side],
            send_sem=res_send.at[k, side],
            recv_sem=res_recv.at[k, side],
            device_id={"lag": outward},
            device_id_type=MESH,
        )

    def target(k, side):
        return EDGE - 1 - k + side * (2 * k + 1)

    barrier = pltpu.get_barrier_semaphore()
    pl.semaphore_signal(barrier, inc=1, device_id={"tile": left}, device_id_type=MESH)
    pl.semaphore_signal(barrier, inc=1, device_id={"tile": right}, device_id_type=MESH)

    @pl.when(lag > 0)
    def _():
        pl.semaphore_signal(barrier, inc=1, device_id={"lag": lag - 1}, device_id_type=MESH)

    @pl.when(lag < n_lag - 1)
    def _():
        pl.semaphore_signal(barrier, inc=1, device_id={"lag": lag + 1}, device_id_type=MESH)

    at_end = (lag == 0) | (lag == n_lag - 1)
    pl.semaphore_wait(barrier, jnp.where(at_end, 3, 4))

    def is_early(c):
        return (c < 2 * (lag + 2)) | ~left_half

    for c in range(here):
        @pl.when((lag < n_lag - 1) & is_early(c))
        def _():
            carry(c).start()

    for l in range(lags):
        for side in range(2):
            halo(0, side, l).start()

    def start_late(part):
        for c in range(part, here, 2):
            @pl.when((lag < n_lag - 1) & ~is_early(c))
            def _():
                carry(c).start()

    loads = [
        pltpu.make_async_copy(history, window.at[:, pl.ds(EDGE, here)], local_sem.at[0]),
        pltpu.make_async_copy(lag_blocks, blocks, local_sem.at[1]),
        pltpu.make_async_copy(self_inverse, inverse, local_sem.at[2]),
        pltpu.make_async_copy(excitation, excite, local_sem.at[3]),
    ]
    for load in loads:
        load.start()
    for l in range(lags):
        @pl.loop(0, vec // ROWS)
        def _(r):
            window[l, here + 2 * EDGE, pl.ds(pl.multiple_of(r * ROWS, ROWS), ROWS)] = jnp.zeros((ROWS, width), window.dtype)
    for load in loads:
        load.wait()
    kept = pltpu.make_async_copy(
        window.at[pl.ds(0, lags - 1), pl.ds(EDGE, here)], older, local_sem.at[4]
    )
    kept.start()

    def compute(k):
        for l in range(lags):
            for side in range(2):
                halo(k, side, l).wait_recv()
                if k + 1 < EDGE:
                    halo(k + 1, side, l).start()
        for l in range(lags):
            @pl.loop(0, vec // ROWS)
            def _(r):
                rows = pl.ds(pl.multiple_of(r * ROWS, ROWS), ROWS)
                window[l, EDGE - 1 - k, rows] = land[k, 0, l, rows]
                window[l, EDGE + here + k, rows] = land[k, 1, l, rows]

        for side in range(2):
            b = target(k, side)

            @pl.loop(0, width // COLS)
            def _(c):
                cols = pl.ds(pl.multiple_of(c * COLS, COLS), COLS)
                lhs, rhs = [], []
                for l in range(lags):
                    for s in range(SLOTS):
                        index = jnp.where(s < live_counts[l, b], b + pattern[l, s, b], here + 2 * EDGE)
                        lhs.append(blocks[l, b, s])
                        rhs.append(window[l, index, :, cols])
                term = jnp.dot(
                    jnp.concatenate(lhs, axis=1), jnp.concatenate(rhs, axis=0),
                    preferred_element_type=jnp.float32,
                )
                psend[k, side, :, cols] = term.astype(psend.dtype)

            @pl.when(~has_out)
            def _():
                send_inward(k, side)

    def send_inward(k, side):
        @pl.when(middle)
        def _():
            to_inward(k, side, resbox, res_recv).start()

        @pl.when(~middle)
        def _():
            to_inward(k, side, inbox, in_recv).start()

    def forward(k, side):
        @pl.when(has_out)
        def _():
            to_inward(k, side, inbox, in_recv).wait_recv()

            @pl.loop(0, vec // ROWS)
            def _(r):
                rows = pl.ds(pl.multiple_of(r * ROWS, ROWS), ROWS)
                psend[k, side, rows] = (
                    psend[k, side, rows].astype(jnp.float32) + inbox[k, side, rows].astype(jnp.float32)
                ).astype(psend.dtype)

            send_inward(k, side)

    def resolve(k, side):
        to_outward(k, side).wait_recv()

        @pl.when(middle)
        def _():
            @pl.loop(0, vec // ROWS)
            def _(r):
                rows = pl.ds(pl.multiple_of(r * ROWS, ROWS), ROWS)
                field = psend[k, side, rows].astype(jnp.float32) + resbox[k, side, rows].astype(jnp.float32)
                resbox[k, side, rows] = (excite[target(k, side), rows] - field).astype(resbox.dtype)

        @pl.when(has_out)
        def _():
            to_outward(k, side).start()

        traction[target(k, side)] = jnp.dot(
            inverse[target(k, side)], resbox[k, side], preferred_element_type=jnp.float32
        ).astype(traction.dtype)

    def resolve_middle(k, side):
        @pl.when(middle)
        def _():
            resolve(k, side)
            if k == EDGE - 1:
                start_late(side)

    for k in range(EDGE):
        if k == EDGE - 1:
            for side in range(2):
                resolve_middle(0, side)
        compute(k)
        for side in range(2):
            if k == EDGE - 1:
                resolve_middle(1, side)
            if k > 0:
                forward(k - 1, side)
    for side in range(2):
        resolve_middle(2, side)
        forward(EDGE - 1, side)
    for side in range(2):
        resolve_middle(EDGE - 1, side)

    @pl.when(~middle)
    def _():
        for side in range(2):
            to_inward(EDGE - 1, side, inbox, in_recv).wait_send()
            start_late(side)
        for k in range(EDGE):
            for side in range(2):
                resolve(k, side)

    kept.wait()
    for k in range(EDGE):
        for side in range(2):
            for l in range(lags):
                halo(k, side, l).wait_send()
            if k < EDGE - 1:
                to_inward(k, side, inbox, in_recv).wait_send()
            else:
                @pl.when(middle)
                def _():
                    to_inward(k, side, inbox, in_recv).wait_send()

            @pl.when(has_out)
            def _():
                to_outward(k, side).wait_send()

    for c in range(here):
        @pl.when(lag < n_lag - 1)
        def _():
            carry(c).wait_send()

        @pl.when(lag > 0)
        def _():
            carry(c).wait_recv()


def place(traction, newest, older, traction_out, shifted_out, sem):
    lags, here = shifted_out.shape[:2]
    first = lax.axis_index("lag") == 0
    for c in range(here):
        pltpu.make_async_copy(traction.at[c], traction_out.at[c], sem.at[0, c]).start()
        for l in range(1, lags):
            pltpu.make_async_copy(older.at[l - 1, c], shifted_out.at[l, c], sem.at[l + 1, c]).start()

        @pl.when(first)
        def _():
            pltpu.make_async_copy(traction.at[c], shifted_out.at[0, c], sem.at[1, c]).start()

        @pl.when(~first)
        def _():
            pltpu.make_async_copy(newest.at[c], shifted_out.at[0, c], sem.at[1, c]).start()

    for c in range(here):
        pltpu.make_async_copy(traction.at[c], traction_out.at[c], sem.at[0, c]).wait()
        for l in range(lags):
            pltpu.make_async_copy(traction.at[c], shifted_out.at[l, c], sem.at[l + 1, c]).wait()


def shards(n_tile, n_lag, history, lag_blocks, self_inverse, excitation, pattern, live_counts):
    lags, here, vec, width = history.shape
    kind = history.dtype
    anywhere = pl.BlockSpec(memory_space=pl.ANY)
    scalars = pl.BlockSpec(memory_space=pltpu.SMEM)
    dma = pltpu.SemaphoreType.DMA
    pair = (EDGE, 2, vec, width)
    flops = 2 * here * vec * vec * width * (lags * SLOTS + 1)
    traction, newest, older = pl.pallas_call(
        functools.partial(march, n_tile, n_lag),
        out_shape=(
            pltpu.VMEM((here, vec, width), kind),
            pltpu.VMEM((here, vec, width), kind),
            pltpu.VMEM((lags - 1, here, vec, width), kind),
        ),
        in_specs=[anywhere] * 4 + [scalars] * 2,
        out_specs=(pl.BlockSpec(memory_space=pltpu.VMEM), anywhere, anywhere),
        scratch_shapes=[
            pltpu.VMEM((lags, here + 2 * EDGE + 1, vec, width), kind),
            pltpu.VMEM((EDGE, 2, lags, vec, width), kind),
            pltpu.VMEM(lag_blocks.shape, kind),
            pltpu.VMEM(self_inverse.shape, kind),
            pltpu.VMEM(excitation.shape, excitation.dtype),
            pltpu.VMEM(pair, kind),
            pltpu.VMEM(pair, kind),
            pltpu.VMEM(pair, kind),
            dma((5,)),
            dma((EDGE, 2, lags)), dma((EDGE, 2, lags)),
            dma((here,)), dma((here,)),
            dma((EDGE, 2)), dma((EDGE, 2)),
            dma((EDGE, 2)), dma((EDGE, 2)),
        ],
        compiler_params=pltpu.CompilerParams(
            collective_id=0, has_side_effects=True, vmem_limit_bytes=54 * 2**20
        ),
        cost_estimate=pl.CostEstimate(flops=flops, bytes_accessed=40 * 2**20, transcendentals=0),
    )(history, lag_blocks, self_inverse, excitation, jnp.swapaxes(pattern, 1, 2), live_counts)
    return pl.pallas_call(
        place,
        out_shape=(
            jax.ShapeDtypeStruct((here, vec, width), kind),
            jax.ShapeDtypeStruct((lags, here, vec, width), kind),
        ),
        in_specs=[anywhere] * 3,
        out_specs=(anywhere, anywhere),
        scratch_shapes=[dma((lags + 1, here))],
        cost_estimate=pl.CostEstimate(flops=0, bytes_accessed=16 * 2**20, transcendentals=0),
    )(traction, newest, older)


def solution(mesh):
    in_specs = (
        P("lag", "tile", None, None),
        P("lag", "tile", None, None, None),
        P("tile", None, None),
        P("tile", None, None),
        P("lag", "tile", None),
        P("lag", "tile"),
    )
    out_specs = (P("tile", None, None), P("lag", "tile", None, None))
    body = functools.partial(shards, mesh.shape["tile"], mesh.shape["lag"])
    return jax.shard_map(body, mesh=mesh, in_specs=in_specs, out_specs=out_specs, check_vma=False)
```

```python
import functools

import jax
import jax.numpy as jnp
from jax import lax
from jax.experimental import pallas as pl
from jax.experimental.pallas import tpu as pltpu
from jax.sharding import PartitionSpec as P

SLOTS = 2
EDGE = 4
COLS = 256
ROWS = 128
MESH = pl.DeviceIdType.MESH


def march(
    n_tile, n_lag,
    history, lag_blocks, self_inverse, excitation, pattern, live_counts,
    traction, newest, older,
    window, land, blocks, inverse, excite, psend, inbox, resbox,
    local_sem, halo_send, halo_recv, carry_send, carry_recv,
    in_send, in_recv, res_send, res_recv,
):
    lags, here, vec, width = history.shape
    tile = lax.axis_index("tile")
    lag = lax.axis_index("lag")
    half = n_lag // 2
    right, left = lax.rem(tile + 1, n_tile), lax.rem(tile + n_tile - 1, n_tile)
    left_half = lag < half
    inward = jnp.where(left_half, lag + 1, lag - 1)
    has_out = (lag > 0) & (lag < n_lag - 1)
    outward = jnp.where(has_out, jnp.where(left_half, lag - 1, lag + 1), inward)
    middle = (lag == half - 1) | (lag == half)

    def halo(k, side, l):
        block = here - 1 - k if side == 0 else k
        return pltpu.make_async_remote_copy(
            src_ref=history.at[l, block],
            dst_ref=land.at[k, side, l],
            send_sem=halo_send.at[k, side, l],
            recv_sem=halo_recv.at[k, side, l],
            device_id={"tile": right if side == 0 else left},
            device_id_type=MESH,
        )

    def carry(c):
        return pltpu.make_async_remote_copy(
            src_ref=history.at[lags - 1, c],
            dst_ref=newest.at[c],
            send_sem=carry_send.at[c],
            recv_sem=carry_recv.at[c],
            device_id={"lag": lax.rem(lag + 1, n_lag)},
            device_id_type=MESH,
        )

    def to_inward(k, side, dst, recv):
        return pltpu.make_async_remote_copy(
            src_ref=psend.at[k, side],
            dst_ref=dst.at[k, side],
            send_sem=in_send.at[k, side],
            recv_sem=recv.at[k, side],
            device_id={"lag": inward},
            device_id_type=MESH,
        )

    def to_outward(k, side):
        return pltpu.make_async_remote_copy(
            src_ref=resbox.at[k, side],
            dst_ref=resbox.at[k, side],
            send_sem=res_send.at[k, side],
            recv_sem=res_recv.at[k, side],
            device_id={"lag": outward},
            device_id_type=MESH,
        )

    def target(k, side):
        return EDGE - 1 - k + side * (2 * k + 1)

    barrier = pltpu.get_barrier_semaphore()
    pl.semaphore_signal(barrier, inc=1, device_id={"tile": left}, device_id_type=MESH)
    pl.semaphore_signal(barrier, inc=1, device_id={"tile": right}, device_id_type=MESH)

    @pl.when(lag > 0)
    def _():
        pl.semaphore_signal(barrier, inc=1, device_id={"lag": lag - 1}, device_id_type=MESH)

    @pl.when(lag < n_lag - 1)
    def _():
        pl.semaphore_signal(barrier, inc=1, device_id={"lag": lag + 1}, device_id_type=MESH)

    at_end = (lag == 0) | (lag == n_lag - 1)
    pl.semaphore_wait(barrier, jnp.where(at_end, 3, 4))

    def is_early(c):
        return (c < 2 * (lag + 2)) | ~left_half

    for c in range(here):
        @pl.when((lag < n_lag - 1) & is_early(c))
        def _():
            carry(c).start()

    for l in range(lags):
        for side in range(2):
            halo(0, side, l).start()

    def start_late(part):
        for c in range(part, here, 2):
            @pl.when((lag < n_lag - 1) & ~is_early(c))
            def _():
                carry(c).start()

    loads = [
        pltpu.make_async_copy(history, window.at[:, pl.ds(EDGE, here)], local_sem.at[0]),
        pltpu.make_async_copy(lag_blocks, blocks, local_sem.at[1]),
        pltpu.make_async_copy(self_inverse, inverse, local_sem.at[2]),
        pltpu.make_async_copy(excitation, excite, local_sem.at[3]),
    ]
    for load in loads:
        load.start()
    for l in range(lags):
        @pl.loop(0, vec // ROWS)
        def _(r):
            window[l, here + 2 * EDGE, pl.ds(pl.multiple_of(r * ROWS, ROWS), ROWS)] = jnp.zeros((ROWS, width), window.dtype)
    for load in loads:
        load.wait()
    kept = pltpu.make_async_copy(
        window.at[pl.ds(0, lags - 1), pl.ds(EDGE, here)], older, local_sem.at[4]
    )
    kept.start()

    def compute(k):
        for l in range(lags):
            for side in range(2):
                halo(k, side, l).wait_recv()
                if k + 1 < EDGE:
                    halo(k + 1, side, l).start()
        for l in range(lags):
            @pl.loop(0, vec // ROWS)
            def _(r):
                rows = pl.ds(pl.multiple_of(r * ROWS, ROWS), ROWS)
                window[l, EDGE - 1 - k, rows] = land[k, 0, l, rows]
                window[l, EDGE + here + k, rows] = land[k, 1, l, rows]

        for side in range(2):
            b = target(k, side)

            @pl.loop(0, width // COLS)
            def _(c):
                cols = pl.ds(pl.multiple_of(c * COLS, COLS), COLS)
                lhs, rhs = [], []
                for l in range(lags):
                    for s in range(SLOTS):
                        index = jnp.where(s < live_counts[l, b], b + pattern[l, s, b], here + 2 * EDGE)
                        lhs.append(blocks[l, b, s])
                        rhs.append(window[l, index, :, cols])
                term = jnp.dot(
                    jnp.concatenate(lhs, axis=1), jnp.concatenate(rhs, axis=0),
                    preferred_element_type=jnp.float32,
                )
                psend[k, side, :, cols] = term.astype(psend.dtype)

            @pl.when(~has_out)
            def _():
                send_inward(k, side)

    def send_inward(k, side):
        @pl.when(middle)
        def _():
            to_inward(k, side, resbox, res_recv).start()

        @pl.when(~middle)
        def _():
            to_inward(k, side, inbox, in_recv).start()

    def forward(k, side):
        @pl.when(has_out)
        def _():
            to_inward(k, side, inbox, in_recv).wait_recv()

            @pl.loop(0, vec // ROWS)
            def _(r):
                rows = pl.ds(pl.multiple_of(r * ROWS, ROWS), ROWS)
                psend[k, side, rows] = (
                    psend[k, side, rows].astype(jnp.float32) + inbox[k, side, rows].astype(jnp.float32)
                ).astype(psend.dtype)

            send_inward(k, side)

    def resolve(k, side):
        to_outward(k, side).wait_recv()

        @pl.when(middle)
        def _():
            @pl.loop(0, vec // ROWS)
            def _(r):
                rows = pl.ds(pl.multiple_of(r * ROWS, ROWS), ROWS)
                field = psend[k, side, rows].astype(jnp.float32) + resbox[k, side, rows].astype(jnp.float32)
                resbox[k, side, rows] = (excite[target(k, side), rows] - field).astype(resbox.dtype)

        @pl.when(has_out)
        def _():
            to_outward(k, side).start()

        traction[target(k, side)] = jnp.dot(
            inverse[target(k, side)], resbox[k, side], preferred_element_type=jnp.float32
        ).astype(traction.dtype)

    def resolve_middle(k, side):
        @pl.when(middle)
        def _():
            resolve(k, side)
            if k == EDGE - 1 and side == 1:
                start_late(0)
                start_late(1)

    for k in range(EDGE):
        if k == EDGE - 1:
            for side in range(2):
                resolve_middle(0, side)
        compute(k)
        for side in range(2):
            if k == EDGE - 1:
                resolve_middle(1, side)
            if k > 0:
                forward(k - 1, side)
    for side in range(2):
        resolve_middle(2, side)
        forward(EDGE - 1, side)
    for side in range(2):
        resolve_middle(EDGE - 1, side)

    @pl.when(~middle)
    def _():
        for side in range(2):
            to_inward(EDGE - 1, side, inbox, in_recv).wait_send()
            start_late(side)
        for k in range(EDGE):
            for side in range(2):
                resolve(k, side)

    kept.wait()
    for k in range(EDGE):
        for side in range(2):
            for l in range(lags):
                halo(k, side, l).wait_send()
            if k < EDGE - 1:
                to_inward(k, side, inbox, in_recv).wait_send()
            else:
                @pl.when(middle)
                def _():
                    to_inward(k, side, inbox, in_recv).wait_send()

            @pl.when(has_out)
            def _():
                to_outward(k, side).wait_send()

    for c in range(here):
        @pl.when(lag < n_lag - 1)
        def _():
            carry(c).wait_send()

        @pl.when(lag > 0)
        def _():
            carry(c).wait_recv()


def place(traction, newest, older, traction_out, shifted_out, sem):
    lags, here = shifted_out.shape[:2]
    first = lax.axis_index("lag") == 0
    for c in range(here):
        pltpu.make_async_copy(traction.at[c], traction_out.at[c], sem.at[0, c]).start()
        for l in range(1, lags):
            pltpu.make_async_copy(older.at[l - 1, c], shifted_out.at[l, c], sem.at[l + 1, c]).start()

        @pl.when(first)
        def _():
            pltpu.make_async_copy(traction.at[c], shifted_out.at[0, c], sem.at[1, c]).start()

        @pl.when(~first)
        def _():
            pltpu.make_async_copy(newest.at[c], shifted_out.at[0, c], sem.at[1, c]).start()

    for c in range(here):
        pltpu.make_async_copy(traction.at[c], traction_out.at[c], sem.at[0, c]).wait()
        for l in range(lags):
            pltpu.make_async_copy(traction.at[c], shifted_out.at[l, c], sem.at[l + 1, c]).wait()


def shards(n_tile, n_lag, history, lag_blocks, self_inverse, excitation, pattern, live_counts):
    lags, here, vec, width = history.shape
    kind = history.dtype
    anywhere = pl.BlockSpec(memory_space=pl.ANY)
    scalars = pl.BlockSpec(memory_space=pltpu.SMEM)
    dma = pltpu.SemaphoreType.DMA
    pair = (EDGE, 2, vec, width)
    flops = 2 * here * vec * vec * width * (lags * SLOTS + 1)
    traction, newest, older = pl.pallas_call(
        functools.partial(march, n_tile, n_lag),
        out_shape=(
            pltpu.VMEM((here, vec, width), kind),
            pltpu.VMEM((here, vec, width), kind),
            pltpu.VMEM((lags - 1, here, vec, width), kind),
        ),
        in_specs=[anywhere] * 4 + [scalars] * 2,
        out_specs=(pl.BlockSpec(memory_space=pltpu.VMEM), anywhere, anywhere),
        scratch_shapes=[
            pltpu.VMEM((lags, here + 2 * EDGE + 1, vec, width), kind),
            pltpu.VMEM((EDGE, 2, lags, vec, width), kind),
            pltpu.VMEM(lag_blocks.shape, kind),
            pltpu.VMEM(self_inverse.shape, kind),
            pltpu.VMEM(excitation.shape, excitation.dtype),
            pltpu.VMEM(pair, kind),
            pltpu.VMEM(pair, kind),
            pltpu.VMEM(pair, kind),
            dma((5,)),
            dma((EDGE, 2, lags)), dma((EDGE, 2, lags)),
            dma((here,)), dma((here,)),
            dma((EDGE, 2)), dma((EDGE, 2)),
            dma((EDGE, 2)), dma((EDGE, 2)),
        ],
        compiler_params=pltpu.CompilerParams(
            collective_id=0, has_side_effects=True, vmem_limit_bytes=54 * 2**20
        ),
        cost_estimate=pl.CostEstimate(flops=flops, bytes_accessed=40 * 2**20, transcendentals=0),
    )(history, lag_blocks, self_inverse, excitation, jnp.swapaxes(pattern, 1, 2), live_counts)
    return pl.pallas_call(
        place,
        out_shape=(
            jax.ShapeDtypeStruct((here, vec, width), kind),
            jax.ShapeDtypeStruct((lags, here, vec, width), kind),
        ),
        in_specs=[pl.BlockSpec(memory_space=pltpu.VMEM)] * 3,
        out_specs=(anywhere, anywhere),
        scratch_shapes=[dma((lags + 1, here))],
        compiler_params=pltpu.CompilerParams(vmem_limit_bytes=32 * 2**20),
        cost_estimate=pl.CostEstimate(flops=0, bytes_accessed=16 * 2**20, transcendentals=0),
    )(traction, newest, older)


def solution(mesh):
    in_specs = (
        P("lag", "tile", None, None),
        P("lag", "tile", None, None, None),
        P("tile", None, None),
        P("tile", None, None),
        P("lag", "tile", None),
        P("lag", "tile"),
    )
    out_specs = (P("tile", None, None), P("lag", "tile", None, None))
    body = functools.partial(shards, mesh.shape["tile"], mesh.shape["lag"])
    return jax.shard_map(body, mesh=mesh, in_specs=in_specs, out_specs=out_specs, check_vma=False)
```

```python
import functools

import jax
import jax.numpy as jnp
from jax import lax
from jax.experimental import pallas as pl
from jax.experimental.pallas import tpu as pltpu
from jax.sharding import PartitionSpec as P

SLOTS = 2
EDGE = 4
COLS = 256
ROWS = 128
MESH = pl.DeviceIdType.MESH


def march(
    n_tile, n_lag,
    history, lag_blocks, self_inverse, excitation, pattern, live_counts,
    traction, newest, older,
    window, land, blocks, inverse, excite, psend, inbox, resbox,
    local_sem, halo_send, halo_recv, carry_send, carry_recv,
    in_send, in_recv, res_send, res_recv,
):
    lags, here, vec, width = history.shape
    tile = lax.axis_index("tile")
    lag = lax.axis_index("lag")
    half = n_lag // 2
    right, left = lax.rem(tile + 1, n_tile), lax.rem(tile + n_tile - 1, n_tile)
    left_half = lag < half
    inward = jnp.where(left_half, lag + 1, lag - 1)
    has_out = (lag > 0) & (lag < n_lag - 1)
    outward = jnp.where(has_out, jnp.where(left_half, lag - 1, lag + 1), inward)
    middle = (lag == half - 1) | (lag == half)

    def halo(k, side, l):
        block = here - 1 - k if side == 0 else k
        return pltpu.make_async_remote_copy(
            src_ref=history.at[l, block],
            dst_ref=land.at[k, side, l],
            send_sem=halo_send.at[k, side, l],
            recv_sem=halo_recv.at[k, side, l],
            device_id={"tile": right if side == 0 else left},
            device_id_type=MESH,
        )

    def carry(c):
        return pltpu.make_async_remote_copy(
            src_ref=history.at[lags - 1, c],
            dst_ref=newest.at[c],
            send_sem=carry_send.at[c],
            recv_sem=carry_recv.at[c],
            device_id={"lag": lax.rem(lag + 1, n_lag)},
            device_id_type=MESH,
        )

    def to_inward(k, side, dst, recv):
        return pltpu.make_async_remote_copy(
            src_ref=psend.at[k, side],
            dst_ref=dst.at[k, side],
            send_sem=in_send.at[k, side],
            recv_sem=recv.at[k, side],
            device_id={"lag": inward},
            device_id_type=MESH,
        )

    def to_outward(k, side):
        return pltpu.make_async_remote_copy(
            src_ref=resbox.at[k, side],
            dst_ref=resbox.at[k, side],
            send_sem=res_send.at[k, side],
            recv_sem=res_recv.at[k, side],
            device_id={"lag": outward},
            device_id_type=MESH,
        )

    def target(k, side):
        return EDGE - 1 - k + side * (2 * k + 1)

    barrier = pltpu.get_barrier_semaphore()
    pl.semaphore_signal(barrier, inc=1, device_id={"tile": left}, device_id_type=MESH)
    pl.semaphore_signal(barrier, inc=1, device_id={"tile": right}, device_id_type=MESH)

    @pl.when(lag > 0)
    def _():
        pl.semaphore_signal(barrier, inc=1, device_id={"lag": lag - 1}, device_id_type=MESH)

    @pl.when(lag < n_lag - 1)
    def _():
        pl.semaphore_signal(barrier, inc=1, device_id={"lag": lag + 1}, device_id_type=MESH)

    at_end = (lag == 0) | (lag == n_lag - 1)
    pl.semaphore_wait(barrier, jnp.where(at_end, 3, 4))

    def is_early(c):
        return (c < 2 * lag + 5) | ~left_half

    for c in range(here):
        @pl.when((lag < n_lag - 1) & is_early(c))
        def _():
            carry(c).start()

    for l in range(lags):
        for side in range(2):
            halo(0, side, l).start()

    def start_late(part):
        for c in range(part, here, 2):
            @pl.when((lag < n_lag - 1) & ~is_early(c))
            def _():
                carry(c).start()

    loads = [
        pltpu.make_async_copy(history, window.at[:, pl.ds(EDGE, here)], local_sem.at[0]),
        pltpu.make_async_copy(lag_blocks, blocks, local_sem.at[1]),
        pltpu.make_async_copy(self_inverse, inverse, local_sem.at[2]),
        pltpu.make_async_copy(excitation, excite, local_sem.at[3]),
    ]
    for load in loads:
        load.start()
    for l in range(lags):
        @pl.loop(0, vec // ROWS)
        def _(r):
            window[l, here + 2 * EDGE, pl.ds(pl.multiple_of(r * ROWS, ROWS), ROWS)] = jnp.zeros((ROWS, width), window.dtype)
    for load in loads:
        load.wait()
    kept = pltpu.make_async_copy(
        window.at[pl.ds(0, lags - 1), pl.ds(EDGE, here)], older, local_sem.at[4]
    )
    kept.start()

    def compute(k):
        for l in range(lags):
            for side in range(2):
                halo(k, side, l).wait_recv()
                if k + 1 < EDGE:
                    halo(k + 1, side, l).start()
        for l in range(lags):
            @pl.loop(0, vec // ROWS)
            def _(r):
                rows = pl.ds(pl.multiple_of(r * ROWS, ROWS), ROWS)
                window[l, EDGE - 1 - k, rows] = land[k, 0, l, rows]
                window[l, EDGE + here + k, rows] = land[k, 1, l, rows]

        for side in range(2):
            b = target(k, side)

            @pl.loop(0, width // COLS)
            def _(c):
                cols = pl.ds(pl.multiple_of(c * COLS, COLS), COLS)
                lhs, rhs = [], []
                for l in range(lags):
                    for s in range(SLOTS):
                        index = jnp.where(s < live_counts[l, b], b + pattern[l, s, b], here + 2 * EDGE)
                        lhs.append(blocks[l, b, s])
                        rhs.append(window[l, index, :, cols])
                term = jnp.dot(
                    jnp.concatenate(lhs, axis=1), jnp.concatenate(rhs, axis=0),
                    preferred_element_type=jnp.float32,
                )
                psend[k, side, :, cols] = term.astype(psend.dtype)

            @pl.when(~has_out)
            def _():
                send_inward(k, side)

    def send_inward(k, side):
        @pl.when(middle)
        def _():
            to_inward(k, side, resbox, res_recv).start()

        @pl.when(~middle)
        def _():
            to_inward(k, side, inbox, in_recv).start()

    def forward(k, side):
        @pl.when(has_out)
        def _():
            to_inward(k, side, inbox, in_recv).wait_recv()

            @pl.loop(0, vec // ROWS)
            def _(r):
                rows = pl.ds(pl.multiple_of(r * ROWS, ROWS), ROWS)
                psend[k, side, rows] = (
                    psend[k, side, rows].astype(jnp.float32) + inbox[k, side, rows].astype(jnp.float32)
                ).astype(psend.dtype)

            send_inward(k, side)

    def resolve(k, side):
        to_outward(k, side).wait_recv()

        @pl.when(middle)
        def _():
            @pl.loop(0, vec // ROWS)
            def _(r):
                rows = pl.ds(pl.multiple_of(r * ROWS, ROWS), ROWS)
                field = psend[k, side, rows].astype(jnp.float32) + resbox[k, side, rows].astype(jnp.float32)
                resbox[k, side, rows] = (excite[target(k, side), rows] - field).astype(resbox.dtype)

        @pl.when(has_out)
        def _():
            to_outward(k, side).start()

        traction[target(k, side)] = jnp.dot(
            inverse[target(k, side)], resbox[k, side], preferred_element_type=jnp.float32
        ).astype(traction.dtype)

    def resolve_middle(k, side):
        @pl.when(middle)
        def _():
            resolve(k, side)
            if k == EDGE - 1:
                start_late(side)

    for k in range(EDGE):
        if k == EDGE - 1:
            for side in range(2):
                resolve_middle(0, side)
        compute(k)
        for side in range(2):
            if k == EDGE - 1:
                resolve_middle(1, side)
            if k > 0:
                forward(k - 1, side)
    for side in range(2):
        resolve_middle(2, side)
        forward(EDGE - 1, side)
    for side in range(2):
        resolve_middle(EDGE - 1, side)

    @pl.when(~middle)
    def _():
        for side in range(2):
            to_inward(EDGE - 1, side, inbox, in_recv).wait_send()
            start_late(side)
        for k in range(EDGE):
            for side in range(2):
                resolve(k, side)

    kept.wait()
    for k in range(EDGE):
        for side in range(2):
            for l in range(lags):
                halo(k, side, l).wait_send()
            if k < EDGE - 1:
                to_inward(k, side, inbox, in_recv).wait_send()
            else:
                @pl.when(middle)
                def _():
                    to_inward(k, side, inbox, in_recv).wait_send()

            @pl.when(has_out)
            def _():
                to_outward(k, side).wait_send()

    for c in range(here):
        @pl.when(lag < n_lag - 1)
        def _():
            carry(c).wait_send()

        @pl.when(lag > 0)
        def _():
            carry(c).wait_recv()


def place(traction, newest, older, traction_out, shifted_out, sem):
    lags, here = shifted_out.shape[:2]
    first = lax.axis_index("lag") == 0
    for c in range(here):
        pltpu.make_async_copy(traction.at[c], traction_out.at[c], sem.at[0, c]).start()
        for l in range(1, lags):
            pltpu.make_async_copy(older.at[l - 1, c], shifted_out.at[l, c], sem.at[l + 1, c]).start()

        @pl.when(first)
        def _():
            pltpu.make_async_copy(traction.at[c], shifted_out.at[0, c], sem.at[1, c]).start()

        @pl.when(~first)
        def _():
            pltpu.make_async_copy(newest.at[c], shifted_out.at[0, c], sem.at[1, c]).start()

    for c in range(here):
        pltpu.make_async_copy(traction.at[c], traction_out.at[c], sem.at[0, c]).wait()
        for l in range(lags):
            pltpu.make_async_copy(traction.at[c], shifted_out.at[l, c], sem.at[l + 1, c]).wait()


def shards(n_tile, n_lag, history, lag_blocks, self_inverse, excitation, pattern, live_counts):
    lags, here, vec, width = history.shape
    kind = history.dtype
    anywhere = pl.BlockSpec(memory_space=pl.ANY)
    scalars = pl.BlockSpec(memory_space=pltpu.SMEM)
    dma = pltpu.SemaphoreType.DMA
    pair = (EDGE, 2, vec, width)
    flops = 2 * here * vec * vec * width * (lags * SLOTS + 1)
    traction, newest, older = pl.pallas_call(
        functools.partial(march, n_tile, n_lag),
        out_shape=(
            pltpu.VMEM((here, vec, width), kind),
            pltpu.VMEM((here, vec, width), kind),
            pltpu.VMEM((lags - 1, here, vec, width), kind),
        ),
        in_specs=[anywhere] * 4 + [scalars] * 2,
        out_specs=(pl.BlockSpec(memory_space=pltpu.VMEM), anywhere, anywhere),
        scratch_shapes=[
            pltpu.VMEM((lags, here + 2 * EDGE + 1, vec, width), kind),
            pltpu.VMEM((EDGE, 2, lags, vec, width), kind),
            pltpu.VMEM(lag_blocks.shape, kind),
            pltpu.VMEM(self_inverse.shape, kind),
            pltpu.VMEM(excitation.shape, excitation.dtype),
            pltpu.VMEM(pair, kind),
            pltpu.VMEM(pair, kind),
            pltpu.VMEM(pair, kind),
            dma((5,)),
            dma((EDGE, 2, lags)), dma((EDGE, 2, lags)),
            dma((here,)), dma((here,)),
            dma((EDGE, 2)), dma((EDGE, 2)),
            dma((EDGE, 2)), dma((EDGE, 2)),
        ],
        compiler_params=pltpu.CompilerParams(
            collective_id=0, has_side_effects=True, vmem_limit_bytes=54 * 2**20
        ),
        cost_estimate=pl.CostEstimate(flops=flops, bytes_accessed=40 * 2**20, transcendentals=0),
    )(history, lag_blocks, self_inverse, excitation, jnp.swapaxes(pattern, 1, 2), live_counts)
    return pl.pallas_call(
        place,
        out_shape=(
            jax.ShapeDtypeStruct((here, vec, width), kind),
            jax.ShapeDtypeStruct((lags, here, vec, width), kind),
        ),
        in_specs=[pl.BlockSpec(memory_space=pltpu.VMEM)] * 3,
        out_specs=(anywhere, anywhere),
        scratch_shapes=[dma((lags + 1, here))],
        compiler_params=pltpu.CompilerParams(vmem_limit_bytes=32 * 2**20),
        cost_estimate=pl.CostEstimate(flops=0, bytes_accessed=16 * 2**20, transcendentals=0),
    )(traction, newest, older)


def solution(mesh):
    in_specs = (
        P("lag", "tile", None, None),
        P("lag", "tile", None, None, None),
        P("tile", None, None),
        P("tile", None, None),
        P("lag", "tile", None),
        P("lag", "tile"),
    )
    out_specs = (P("tile", None, None), P("lag", "tile", None, None))
    body = functools.partial(shards, mesh.shape["tile"], mesh.shape["lag"])
    return jax.shard_map(body, mesh=mesh, in_specs=in_specs, out_specs=out_specs, check_vma=False)
```
